32 devices in a mesh: req: 16 (over z, y, x), tp: 2 (over core).
Axes of the slice: x: 2, y: 2, z: 4, core: 2. Of those that a mesh axis runs over, the one named last changes fastest.
Arguments:
- residual: bfloat16 [512, 2048], P('req'), may hold values from -6 to 6
- fresh_qkv: bfloat16 [512, 3, 2048], P('req', None, 'tp'), may hold values from -32 to 32
- kv_cache: bfloat16 [512, 24, 2, 2048], P('req', None, None, 'tp'), may hold values from -32 to 32
- cache_len: int32 [512], P('req'), may hold values from 2 to 24, as said below
- out_proj: bfloat16 [2048, 2048], P('tp'), may hold values from -0.125 to 0.125
- norm_gain: float32 [2048], replicated, may hold values from 0.1 to 1.9
- router_weight: float32 [2048, 16], replicated, may hold values from -7.9549513 to 7.9549513
- expert_ids: int32 [512, 8], P('req'), may hold values from 0 to 15, all different within a row; in each aligned block of 32 rows (0 to 31, 32 to 63, ...) at most 32 rows name the same one
- gate_up: bfloat16 [16, 2048, 2, 1024], P('req', None, None, 'tp'), may hold values from -0.125 to 0.125
- down_proj: bfloat16 [16, 1024, 2048], P('req', 'tp'), may hold values from -0.1875 to 0.1875
Outputs:
- layer_out: bfloat16 [512, 2048], P('req', 'tp')
The draws below stay inside these ranges and needn't reach their ends.
Inputs may be any that keep to these rules, and one draw needn't show every extreme that they name: `expert_ids`: each row names 8 different experts; among the 32 rows of one device no expert is named by more than 32 rows, and some device reaches 32. `cache_len`: some request uses all 24 positions.
All inputs are finite; a program needn't handle non-finite values.
Results may differ from the reference program's by a relative error of at most 0.018.
Values may be sent and summed in bfloat16 or wider, within the bound.
A program may use at most 128 MiB of HBM per device.

```python
import math
import jax
import jax.numpy as jnp
import numpy as np
from jax import lax

D = 2048
H = 16
HD = 128
FF = 1024
TOP = 8
REQS = 32
CL = 24
EXPERTS = 16
CAP = 32
REQTOT = 512
N_REQ = 16


def draw_fresh_qkv(key, part):
    values = jnp.clip(jax.random.normal(jax.random.fold_in(key, 1), (REQTOT, 3, H * HD), jnp.float32), -6.0, 6.0)
    return values.astype(jnp.bfloat16)


def draw_kv_cache(key, part):
    values = jnp.clip(jax.random.normal(jax.random.fold_in(key, 3), (REQTOT, CL, 2, H * HD), jnp.float32), -6.0, 6.0)
    return values.astype(jnp.bfloat16)


def draw_cache_len(key, part):
    lengths = jax.random.randint(jax.random.fold_in(key, 5), (REQTOT,), 2, CL + 1, jnp.int32)
    chosen_spot = jax.random.randint(jax.random.fold_in(key, 6), (), 0, REQTOT, jnp.int32)
    return jnp.where(jnp.arange(REQTOT, dtype=jnp.int32) == chosen_spot, CL, lengths).astype(jnp.int32)


def draw_router_weight(key, part):
    values = jnp.clip(jax.random.normal(jax.random.fold_in(key, 9), (D, EXPERTS), jnp.float32), -6.0, 6.0) * D ** (-0.5)
    return values.astype(jnp.float32)


def levels(stream_key, dims, split, low, top_value):
    loudness, own = 1.0, jax.random.fold_in(stream_key, 6)
    for dim, shards_of in split:
        heights = jnp.exp(jax.random.uniform(jax.random.fold_in(own, dim), (shards_of,), jnp.float32, low / len(split), top_value / len(split)))
        loudness = loudness * jnp.repeat(heights, dims[dim] // shards_of).reshape([-1 if axis == dim else 1 for axis in range(len(dims))])
    return loudness


def shared_out(stream_key, own, number, rows, number_of, top, reach, skew):
    ranking = jax.random.permutation(stream_key, number_of)
    crowded, usual = shares(number_of, rows * top, reach, skew, True), shares(number_of, rows * top, reach, skew, False)
    places = jnp.arange(number_of)

    def named(sizes, turn):
        used = int((sizes > 0).sum())
        fixed = max(1, used // 4)
        passed = fixed + (places - fixed + turn * (used - fixed)) % max(1, number_of - fixed)
        return jnp.zeros((number_of,), jnp.int32).at[ranking[jnp.where(places < fixed, places, passed)]].set(jnp.asarray(sizes, jnp.int32))

    sizes = jnp.where(number % 4 == 0, named(crowded, number // 4), named(usual, number - number // 4 - 1))
    mixed = jax.random.permutation(jax.random.fold_in(own, 3), number_of)
    giver, sink = mixed[0:number_of // 2 * 2:2], mixed[1:number_of // 2 * 2:2]
    margin = jnp.minimum(sizes[giver] - 1, reach - sizes[sink]) // 2
    margin = jnp.where((giver == ranking[0]) | (sink == ranking[0]) | (sizes[sink] == 0), 0, jnp.maximum(margin, 0))
    passed = jax.random.randint(jax.random.fold_in(own, 4), (number_of // 2,), 0, 1 << 20) % (margin + 1)
    sizes = sizes.at[giver].add(-passed).at[sink].add(passed)
    members = jnp.searchsorted(jnp.cumsum(sizes), jnp.arange(rows * top), side="right").astype(jnp.int32)
    listing = members.reshape(top, rows).T
    listing = listing[jax.random.permutation(jax.random.fold_in(own, 1), rows)]
    turn = jax.random.randint(jax.random.fold_in(own, 2), (rows, 1), 0, top)
    return jnp.take_along_axis(listing, (jnp.arange(top)[None, :] + turn) % top, axis=1)


def shares(count, total, most, lean, full):
    loads = [(1 << 20) // math.isqrt(rank ** lean) + 1 for rank in range(1, count + 1)]
    largest = most if full else min(most, max(-(-total // count), total * loads[0] // sum(loads)))
    least = 1 if total - largest >= count - 1 else 0
    given, spare = [largest] + [least] * (count - 1), total - largest - least * (count - 1)
    while spare > 0:
        candidates = [i for i in range(1, count) if given[i] < largest] or [i for i in range(1, count) if given[i] < most]
        whole, remaining = sum([loads[i] for i in candidates]), spare
        for i in candidates:
            addition = min(most - given[i], max(1, remaining * loads[i] // whole), spare)
            given[i] = given[i] + addition
            spare = spare - addition
    return np.array(given)


def centred(rng, dims, scale, reach, split=(), kind=jnp.bfloat16):
    entries = jax.random.normal(rng, dims, jnp.float32) * scale
    if len(split) > 0:
        entries = levels(rng, dims, split, -0.22, 0.18) * entries
    return jnp.clip(entries, min=-reach, max=reach).astype(kind)


def setup_inputs(seed: int = 0) -> dict:
    arg_keys = jax.random.split(jax.random.key(seed), 11)
    residual = centred(arg_keys[0], (REQTOT, D), 1.0, 6.0, ((0, 16),))
    fresh_qkv = draw_fresh_qkv(jax.random.fold_in(arg_keys[10], 71), 0)
    kv_cache = draw_kv_cache(jax.random.fold_in(arg_keys[10], 71), 0)
    cache_len = draw_cache_len(jax.random.fold_in(arg_keys[10], 71), 0)
    out_proj = centred(arg_keys[4], (H * HD, D), (H * HD) ** -0.5, 0.125, ((0, 2),))
    norm_gain = jnp.clip(1.0 + 0.18 * jax.random.normal(arg_keys[5], (D,), jnp.float32), 0.1, 1.9)
    router_weight = draw_router_weight(jax.random.fold_in(arg_keys[10], 71), 0)
    expert_ids_keys = jax.random.split(jax.random.fold_in(arg_keys[7], 1), REQTOT // REQS)
    expert_ids_turns = jax.random.permutation(jax.random.fold_in(arg_keys[7], 3), REQTOT // REQS)
    expert_ids = jax.vmap(lambda own, number: shared_out(jax.random.fold_in(arg_keys[7], 2), own, number, REQS, EXPERTS, TOP, CAP, 2))(expert_ids_keys, expert_ids_turns).reshape((REQTOT, TOP))
    gate_up = centred(arg_keys[8], (EXPERTS, D, 2, FF), D ** -0.5, 0.125, ((0, 16), (3, 2)))
    down_proj = centred(arg_keys[9], (EXPERTS, FF, D), FF ** -0.5, 0.1875, ((0, 16), (1, 2)))
    return dict(residual=residual, fresh_qkv=fresh_qkv, kv_cache=kv_cache, cache_len=cache_len, out_proj=out_proj, norm_gain=norm_gain, router_weight=router_weight, expert_ids=expert_ids, gate_up=gate_up, down_proj=down_proj)


def rms_normed(hidden_in, gain):
    values = hidden_in.astype(jnp.float32)
    scale_inv = lax.rsqrt(lax.optimization_barrier(jnp.mean(values * values, axis=-1, keepdims=True)) + 1e-05)
    return (values * scale_inv * gain).astype(jnp.bfloat16)

def reference(residual, fresh_qkv, kv_cache, cache_len, out_proj, norm_gain, router_weight, expert_ids, gate_up, down_proj):
    count = residual.shape[0]
    queries = fresh_qkv[:, 0].astype(jnp.float32).reshape(count, H, HD)
    new_keys = fresh_qkv[:, 1].astype(jnp.float32).reshape(count, H, HD)
    new_values = fresh_qkv[:, 2].astype(jnp.float32).reshape(count, H, HD)
    cache_keys = kv_cache[:, :, 0].astype(jnp.float32).reshape(count, CL, H, HD)
    cache_values = kv_cache[:, :, 1].astype(jnp.float32).reshape(count, CL, H, HD)
    factor = HD ** (-0.5)
    scores = jnp.einsum('nhd,nchd->nhc', queries, cache_keys) * factor
    own_score = lax.optimization_barrier(jnp.sum(queries * new_keys, axis=-1)) * factor
    valid = (jnp.arange(CL, dtype=jnp.int32)[None, :] < cache_len[:, None])[:, None, :]
    masked = jnp.where(valid, scores, -jnp.inf)
    top_score = jnp.maximum(lax.optimization_barrier(jnp.max(masked, axis=-1)), own_score)
    expos = jnp.where(valid, jnp.exp(masked - top_score[..., None]), 0.0)
    own_expo = jnp.exp(own_score - top_score)
    total = lax.optimization_barrier(jnp.sum(expos, axis=-1)) + own_expo
    weights = (expos / total[..., None]).astype(jnp.bfloat16)
    own_weight = (own_expo / total).astype(jnp.bfloat16)
    mixed = jnp.einsum('nhc,nchd->nhd', weights.astype(jnp.float32), cache_values)
    mixed = mixed + own_weight.astype(jnp.float32)[..., None] * new_values
    attended = mixed.astype(jnp.bfloat16).reshape(count, H * HD)
    hidden = (residual.astype(jnp.float32) + jnp.dot(attended, out_proj, preferred_element_type=jnp.float32)).astype(jnp.bfloat16)
    normed = rms_normed(hidden, norm_gain)
    logits = jnp.dot(normed.astype(jnp.float32), router_weight, precision=lax.Precision.HIGHEST)
    chosen = jnp.take_along_axis(logits, expert_ids, axis=1)
    gate_vals = jax.nn.softmax(chosen, axis=-1)
    onehot = (expert_ids[:, :, None] == jnp.arange(EXPERTS, dtype=jnp.int32)[None, None, :]).astype(jnp.int32)
    onehot = onehot.reshape(N_REQ, REQS * TOP, EXPERTS)
    running = jnp.cumsum(onehot, axis=1)
    slot_index = (lax.optimization_barrier(jnp.sum(running * onehot, axis=-1)) - 1).reshape(-1)
    source = jnp.arange(count * TOP, dtype=jnp.int32) // (REQS * TOP)
    flat_ids = expert_ids.reshape(-1)
    per_expert = N_REQ * CAP
    position = (flat_ids * per_expert + source * CAP + slot_index).astype(jnp.int32)
    buffer = jnp.zeros((EXPERTS * per_expert, D), jnp.bfloat16).at[position].set(jnp.repeat(normed, TOP, axis=0))

    def one_expert(expert):
        block = lax.dynamic_slice_in_dim(buffer, expert * per_expert, per_expert, 0)
        both = jnp.dot(block, gate_up[expert].reshape(D, 2 * FF), preferred_element_type=jnp.float32).reshape(per_expert, 2, FF)
        inner = (jax.nn.silu(both[:, 0]) * both[:, 1]).astype(jnp.bfloat16)
        return jnp.dot(inner, down_proj[expert], preferred_element_type=jnp.float32)
    results = lax.map(one_expert, jnp.arange(EXPERTS, dtype=jnp.int32)).reshape(EXPERTS * per_expert, D)
    picked = results[position].reshape(count, TOP, D)
    moe_sum = lax.optimization_barrier(jnp.sum(gate_vals[:, :, None] * picked, axis=1))
    return (hidden.astype(jnp.float32) + moe_sum).astype(jnp.bfloat16)
```

```python
import jax
import jax.numpy as jnp
from jax import lax
from jax.sharding import PartitionSpec as P

HD = 128


def rms_normed(hidden_in, gain):
    values = hidden_in.astype(jnp.float32)
    scale_inv = lax.rsqrt(jnp.mean(values * values, axis=-1, keepdims=True) + 1e-05)
    return (values * scale_inv * gain).astype(jnp.bfloat16)


def attend(fresh_qkv, kv_cache, cache_len):
    requests, ctx_len = kv_cache.shape[0], kv_cache.shape[1]
    local_heads = fresh_qkv.shape[2] // HD
    queries = fresh_qkv[:, 0].reshape(requests, local_heads, HD)
    new_keys = fresh_qkv[:, 1].reshape(requests, local_heads, HD)
    new_values = fresh_qkv[:, 2].reshape(requests, local_heads, HD)
    cache_keys = kv_cache[:, :, 0].reshape(requests, ctx_len, local_heads, HD)
    cache_values = kv_cache[:, :, 1].reshape(requests, ctx_len, local_heads, HD)
    factor = HD ** (-0.5)
    scores = (
        jnp.einsum("nhd,nchd->nhc", queries, cache_keys, preferred_element_type=jnp.float32)
        * factor
    )
    own_score = (
        jnp.einsum("nhd,nhd->nh", queries, new_keys, preferred_element_type=jnp.float32) * factor
    )
    valid = (jnp.arange(ctx_len, dtype=jnp.int32)[None, :] < cache_len[:, None])[:, None, :]
    masked = jnp.where(valid, scores, -jnp.inf)
    top_score = jnp.maximum(jnp.max(masked, axis=-1), own_score)
    expos = jnp.where(valid, jnp.exp(masked - top_score[..., None]), 0.0)
    own_expo = jnp.exp(own_score - top_score)
    total = jnp.sum(expos, axis=-1) + own_expo
    weights = (expos / total[..., None]).astype(jnp.bfloat16)
    own_weight = (own_expo / total).astype(jnp.bfloat16)
    mixed = jnp.einsum("nhc,nchd->nhd", weights, cache_values, preferred_element_type=jnp.float32)
    mixed = mixed + own_weight.astype(jnp.float32)[..., None] * new_values.astype(jnp.float32)
    return mixed.astype(jnp.bfloat16).reshape(requests, local_heads * HD)


def local(
    residual,
    fresh_qkv,
    kv_cache,
    cache_len,
    out_proj,
    norm_gain,
    router_weight,
    expert_ids,
    gate_up,
    down_proj,
):
    tp_place = lax.axis_index("tp")
    me = lax.axis_index("req")
    experts = lax.axis_size("req")
    attended = attend(fresh_qkv, kv_cache, cache_len)
    partial_value = jnp.dot(attended, out_proj, preferred_element_type=jnp.float32)
    summed = lax.psum(partial_value, "tp")
    hidden = (residual.astype(jnp.float32) + summed).astype(jnp.bfloat16)
    normed = rms_normed(hidden, norm_gain)
    rows = lax.all_gather(normed, "req", axis=0, tiled=True)
    logits = jnp.dot(normed.astype(jnp.float32), router_weight, precision=lax.Precision.HIGHEST)
    named = jnp.any(
        expert_ids[:, :, None] == jnp.arange(experts, dtype=jnp.int32)[None, None, :], axis=1
    )
    gates = jax.nn.softmax(jnp.where(named, logits, -jnp.inf), axis=-1)
    gates_all = lax.all_gather(gates, "req", axis=0, tiled=True)
    mine = jnp.arange(experts, dtype=jnp.int32)[None, :] == me
    weight = jnp.sum(jnp.where(mine, gates_all, 0.0), axis=1, keepdims=True)
    gate_part = jnp.dot(rows, gate_up[0, :, 0], preferred_element_type=jnp.float32)
    up_part = jnp.dot(rows, gate_up[0, :, 1], preferred_element_type=jnp.float32)
    inner = (jax.nn.silu(gate_part) * up_part).astype(jnp.bfloat16)
    result = jnp.dot(inner, down_proj[0], preferred_element_type=jnp.float32)
    own = lax.psum_scatter(result * weight, "tp", scatter_dimension=1, tiled=True)
    moe_share = lax.psum_scatter(own, "req", scatter_dimension=0, tiled=True)
    width_here = moe_share.shape[1]
    own_cols = lax.dynamic_slice_in_dim(hidden, tp_place * width_here, width_here, 1)
    return (own_cols.astype(jnp.float32) + moe_share).astype(jnp.bfloat16)


def solution(mesh):
    in_specs = (
        P("req", None),
        P("req", None, "tp"),
        P("req", None, None, "tp"),
        P("req"),
        P("tp", None),
        P(),
        P(),
        P("req", None),
        P("req", None, None, "tp"),
        P("req", "tp", None),
    )
    out_specs = P("req", "tp")
    return jax.shard_map(local, mesh=mesh, in_specs=in_specs, out_specs=out_specs, check_vma=False)
```

```python
import functools

import jax
import jax.numpy as jnp
from jax import lax
from jax.experimental import pallas as pl
from jax.experimental.pallas import tpu as pltpu
from jax.sharding import PartitionSpec as P

HD = 128


def attend(fresh_qkv, kv_cache, cache_len):
    requests, ctx_len = kv_cache.shape[0], kv_cache.shape[1]
    local_heads = fresh_qkv.shape[2] // HD
    queries = fresh_qkv[:, 0].reshape(requests, local_heads, HD)
    new_keys = fresh_qkv[:, 1].reshape(requests, local_heads, HD)
    new_values = fresh_qkv[:, 2].reshape(requests, local_heads, HD)
    cache_keys = kv_cache[:, :, 0].reshape(requests, ctx_len, local_heads, HD)
    cache_values = kv_cache[:, :, 1].reshape(requests, ctx_len, local_heads, HD)
    factor = HD ** (-0.5)
    scores = (
        jnp.einsum("nhd,nchd->nhc", queries, cache_keys, preferred_element_type=jnp.float32)
        * factor
    )
    own_score = (
        jnp.einsum("nhd,nhd->nh", queries, new_keys, preferred_element_type=jnp.float32) * factor
    )
    valid = (jnp.arange(ctx_len, dtype=jnp.int32)[None, :] < cache_len[:, None])[:, None, :]
    masked = jnp.where(valid, scores, -jnp.inf)
    top_score = jnp.maximum(jnp.max(masked, axis=-1), own_score)
    expos = jnp.where(valid, jnp.exp(masked - top_score[..., None]), 0.0)
    own_expo = jnp.exp(own_score - top_score)
    total = jnp.sum(expos, axis=-1) + own_expo
    weights = (expos / total[..., None]).astype(jnp.bfloat16)
    own_weight = (own_expo / total).astype(jnp.bfloat16)
    mixed = jnp.einsum("nhc,nchd->nhd", weights, cache_values, preferred_element_type=jnp.float32)
    mixed = mixed + own_weight.astype(jnp.float32)[..., None] * new_values.astype(jnp.float32)
    return mixed.astype(jnp.bfloat16).reshape(requests, local_heads * HD)


def moe_kernel(
    deep,
    plane,
    cores,
    partial,
    residual,
    gain,
    router,
    named,
    gate_hbm,
    up_hbm,
    down_hbm,
    out,
    parts,
    hidden,
    normed,
    gathered,
    gate_w,
    up_w,
    down_w,
    core_out,
    core_in,
    plane_out,
    plane_in,
    deep_out,
    deep_in,
    load_sem,
    parts_send,
    parts_recv,
    own_send,
    pass_send,
    slot_recv,
    cross_send,
    cross_recv,
    core_send,
    core_recv,
    plane_send,
    plane_recv,
    deep_send,
    deep_recv,
):
    me = lax.axis_index("req")
    core = lax.axis_index("tp")
    level = me // plane
    place = lax.rem(me, plane)
    tokens, width = residual.shape
    cols = width // cores
    f32, bf16 = jnp.float32, jnp.bfloat16

    loads = [
        pltpu.make_async_copy(src, dst, load_sem.at[i])
        for i, (src, dst) in enumerate(((gate_hbm, gate_w), (up_hbm, up_w), (down_hbm, down_w)))
    ]
    for load in loads:
        load.start()

    def core_at(i):
        return lax.rem(core + i, cores)

    def level_at(i):
        return lax.rem(level + i, deep)

    def place_at(i):
        return lax.rem(place + i, plane)

    barrier = pltpu.get_barrier_semaphore()
    greeted = [(me, core_at(i)) for i in range(1, cores)]
    greeted += [(level_at(i) * plane + place, core) for i in range(1, deep)]
    greeted += [(level * plane + place_at(i), core) for i in range(1, plane)]
    for device in greeted:
        pl.semaphore_signal(barrier, inc=1, device_id=device, device_id_type=pl.DeviceIdType.MESH)
    pl.semaphore_wait(barrier, len(greeted))

    def send(src, dst, send_sem, recv_sem, device):
        copy = pltpu.make_async_remote_copy(
            src_ref=src,
            dst_ref=dst,
            send_sem=send_sem,
            recv_sem=recv_sem,
            device_id=device,
            device_id_type=pl.DeviceIdType.MESH,
        )
        copy.start()
        started.append(copy)

    def arrived(dst, recv_sem):
        pltpu.make_async_copy(dst, dst, recv_sem).wait()

    started = []
    for i in range(1, cores):
        send(partial, parts.at[i - 1], parts_send.at[i - 1], parts_recv.at[i - 1], (me, core_at(i)))
    for i in range(1, cores):
        arrived(parts.at[i - 1], parts_recv.at[i - 1])
    summed = partial[...]
    for i in range(1, cores):
        summed = summed + parts[i - 1]
    hidden[...] = (residual[...].astype(f32) + summed).astype(bf16)
    values = hidden[...].astype(f32)
    scale_inv = lax.rsqrt(jnp.mean(values * values, axis=-1, keepdims=True) + 1e-05)
    normed[...] = (values * scale_inv * gain[...]).astype(bf16)
    logits = jnp.dot(
        normed[...].astype(f32),
        router[...],
        precision=lax.Precision.HIGHEST,
        preferred_element_type=f32,
    )
    half = router.shape[1] // 2
    lane = lax.broadcasted_iota(jnp.int32, logits.shape, 1)
    chosen = named[...] > 0.0
    top = jnp.max(jnp.where(chosen, logits, -jnp.inf), axis=1, keepdims=True)
    expos = jnp.where(chosen, jnp.exp(jnp.where(chosen, logits, top) - top), 0.0)
    total = jnp.sum(jnp.where(lane < half, expos, 0.0), axis=1, keepdims=True)
    gates = expos / total
    high = gates.astype(bf16).astype(f32)
    own_cols = pl.ds(pl.multiple_of(core * cols, 128), cols)
    gathered[core, me, :, 0:cols] = normed[:, own_cols]
    gathered[core, me, :, cols:] = jnp.where(lane < half, high, gates - high).astype(bf16)

    def spread(k):
        slot = level_at(deep - k) * plane + place if k else me
        block = gathered.at[core, slot]
        for j in range(1, plane):
            send(
                block,
                block,
                pass_send.at[k, j - 1],
                slot_recv.at[slot],
                (level * plane + place_at(j), core),
            )

    def cross(k, j):
        slot = level_at(deep - k) * plane + place_at(j)
        block = gathered.at[core, slot]
        for i in range(1, cores):
            send(
                block,
                block,
                cross_send.at[k, j, i - 1],
                cross_recv.at[i - 1, slot],
                (me, core_at(i)),
            )

    mine = gathered.at[core, me]
    for i in range(1, deep):
        send(mine, mine, own_send.at[i - 1], slot_recv.at[me], (level_at(i) * plane + place, core))
    spread(0)
    cross(0, 0)
    for k in range(1, deep):
        slot = level_at(deep - k) * plane + place
        arrived(gathered.at[core, slot], slot_recv.at[slot])
        spread(k)
        cross(k, 0)

    def collect(k):
        first = level_at(deep - k) * plane
        for j in range(1, plane):
            slot = first + place_at(j)
            arrived(gathered.at[core, slot], slot_recv.at[slot])
            cross(k, j)
        for i in range(1, cores):
            for j in range(plane):
                slot = first + place_at(j)
                arrived(gathered.at[core_at(cores - i), slot], cross_recv.at[i - 1, slot])

    def work(k):
        slots = pl.ds(level_at(deep - k) * plane, plane)
        gate_part = up_part = 0.0
        for t in range(cores):
            block = gathered[t, slots, :, 0:cols].reshape(plane * tokens, cols)
            span = slice(t * cols, (t + 1) * cols)
            gate_part += jnp.dot(block, gate_w[span, :], preferred_element_type=f32)
            up_part += jnp.dot(block, up_w[span, :], preferred_element_type=f32)
        inner = (gate_part * (1.0 / (1.0 + jnp.exp(-gate_part))) * up_part).astype(bf16)
        extra = gathered[0, slots, :, cols:].reshape(plane * tokens, 2 * half).astype(f32)
        spot = lax.broadcasted_iota(jnp.int32, extra.shape, 1)
        weight = jnp.sum(
            jnp.where((spot == me) | (spot == me + half), extra, 0.0), axis=1, keepdims=True
        )
        for i in range(1, cores + 1):
            span = pl.ds(pl.multiple_of(core_at(i) * cols, 128), cols)
            result = jnp.dot(inner, down_w[:, span], preferred_element_type=f32) * weight
            core_out[k, i - 1] = result.astype(core_out.dtype).reshape(plane, tokens, cols)
            if i < cores:
                send(
                    core_out.at[k, i - 1],
                    core_in.at[k, i - 1],
                    core_send.at[k, i - 1],
                    core_recv.at[k, i - 1],
                    (me, core_at(i)),
                )

    def over_plane(k):
        for i in range(1, cores):
            arrived(core_in.at[k, i - 1], core_recv.at[k, i - 1])
        for j in list(range(1, plane)) + [0]:
            whole = core_out[k, cores - 1, place_at(j)].astype(f32)
            for i in range(1, cores):
                whole = whole + core_in[k, i - 1, place_at(j)].astype(f32)
            plane_out[k, j] = whole.astype(bf16)
            if j:
                send(
                    plane_out.at[k, j],
                    plane_in.at[k, j - 1],
                    plane_send.at[k, j - 1],
                    plane_recv.at[k, j - 1],
                    (level * plane + place_at(j), core),
                )

    def over_deep(k):
        whole = plane_out[k, 0].astype(f32)
        for j in range(1, plane):
            arrived(plane_in.at[k, j - 1], plane_recv.at[k, j - 1])
            whole = whole + plane_in[k, j - 1].astype(f32)
        if k:
            deep_out[k - 1] = whole.astype(bf16)
            send(
                deep_out.at[k - 1],
                deep_in.at[k - 1],
                deep_send.at[k - 1],
                deep_recv.at[k - 1],
                (level_at(deep - k) * plane + place, core),
            )
        return whole

    own_sum = None
    for step in range(deep + 2):
        if step < deep:
            collect(step)
            if step == 0:
                for load in loads:
                    load.wait()
            work(step)
        if 1 <= step <= deep:
            over_plane(step - 1)
        if step >= 2:
            found = over_deep(step - 2)
            own_sum = found if step == 2 else own_sum
    for k in range(1, deep):
        arrived(deep_in.at[k - 1], deep_recv.at[k - 1])
        own_sum = own_sum + deep_in[k - 1].astype(f32)
    out[...] = (hidden[:, own_cols].astype(f32) + own_sum).astype(bf16)
    for copy in started:
        copy.wait_send()


def moe_call(partial, residual, gain, router, named, gate_w, up_w, down_w):
    shards, cores = lax.axis_size("req"), lax.axis_size("tp")
    deep = 4
    plane = shards // deep
    tokens, width = residual.shape
    units = down_w.shape[0]
    cols = width // cores
    bf16, dma = jnp.bfloat16, pltpu.SemaphoreType.DMA
    others = cores - 1
    vmem = pl.BlockSpec(memory_space=pltpu.VMEM)
    hbm = pl.BlockSpec(memory_space=pl.ANY)
    return pl.pallas_call(
        functools.partial(moe_kernel, deep, plane, cores),
        out_shape=jax.ShapeDtypeStruct((tokens, cols), bf16),
        in_specs=[vmem] * 5 + [hbm] * 3,
        out_specs=vmem,
        scratch_shapes=[
            pltpu.VMEM((others, tokens, width), jnp.float32),
            pltpu.VMEM((tokens, width), bf16),
            pltpu.VMEM((tokens, width), bf16),
            pltpu.VMEM((cores, shards, tokens, cols + router.shape[1]), bf16),
            pltpu.VMEM((width, units), bf16),
            pltpu.VMEM((width, units), bf16),
            pltpu.VMEM((units, width), bf16),
            pltpu.VMEM((deep, cores, plane, tokens, cols), bf16),
            pltpu.VMEM((deep, others, plane, tokens, cols), bf16),
            pltpu.VMEM((deep, plane, tokens, cols), bf16),
            pltpu.VMEM((deep, plane - 1, tokens, cols), bf16),
            pltpu.VMEM((deep - 1, tokens, cols), bf16),
            pltpu.VMEM((deep - 1, tokens, cols), bf16),
            dma((3,)),
            dma((others,)),
            dma((others,)),
            dma((deep - 1,)),
            dma((deep, plane - 1)),
            dma((shards,)),
            dma((deep, plane, others)),
            dma((others, shards)),
            dma((deep, others)),
            dma((deep, others)),
            dma((deep, plane - 1)),
            dma((deep, plane - 1)),
            dma((deep - 1,)),
            dma((deep - 1,)),
        ],
        compiler_params=pltpu.CompilerParams(
            collective_id=0, has_side_effects=True, vmem_limit_bytes=56 * 1024 * 1024
        ),
    )(partial, residual, gain, router, named, gate_w, up_w, down_w)


def local(
    residual,
    fresh_qkv,
    kv_cache,
    cache_len,
    out_proj,
    norm_gain,
    router_weight,
    expert_ids,
    gate_up,
    down_proj,
):
    experts = lax.axis_size("req")
    attended = attend(fresh_qkv, kv_cache, cache_len)
    partial_value = jnp.dot(attended, out_proj, preferred_element_type=jnp.float32)
    half = 64 * (-(-experts // 64))
    lanes = lax.rem(jnp.arange(2 * half, dtype=jnp.int32), half)
    named = jnp.any(expert_ids[:, :, None] == lanes[None, None, :], axis=1).astype(jnp.float32)
    router = jnp.pad(router_weight, ((0, 0), (0, half - experts)))
    router = jnp.concatenate([router, router], axis=1)
    return moe_call(
        partial_value,
        residual,
        norm_gain[None, :],
        router,
        named,
        gate_up[0, :, 0],
        gate_up[0, :, 1],
        down_proj[0],
    )


def solution(mesh):
    in_specs = (
        P("req", None),
        P("req", None, "tp"),
        P("req", None, None, "tp"),
        P("req"),
        P("tp", None),
        P(),
        P(),
        P("req", None),
        P("req", None, None, "tp"),
        P("req", "tp", None),
    )
    out_specs = P("req", "tp")
    return jax.shard_map(local, mesh=mesh, in_specs=in_specs, out_specs=out_specs, check_vma=False)
```

```python
import functools

import jax
import jax.numpy as jnp
from jax import lax
from jax.experimental import pallas as pl
from jax.experimental.pallas import tpu as pltpu
from jax.sharding import PartitionSpec as P

HD = 128


def attend_kernel(ctx_len, lens, q_ref, k_ref, v_ref, kv, proj_hbm, out, proj, attended, scores, load_sem):
    step = pl.program_id(0)
    load = pltpu.make_async_copy(proj_hbm, proj, load_sem)

    @pl.when(step == 0)
    def _():
        load.start()

    f32, bf16 = jnp.float32, jnp.bfloat16
    block, width = q_ref.shape
    pair = 2 * HD
    row = lax.broadcasted_iota(jnp.int32, (pair, pair), 0) // HD
    column = lax.broadcasted_iota(jnp.int32, (pair, pair), 1) // HD
    ones = jnp.where(row == column, 1.0, 0.0).astype(bf16)
    factor = HD ** (-0.5)

    def head_sums(product):
        high = product.astype(bf16)
        low = (product - high.astype(f32)).astype(bf16)
        return jnp.concatenate(
            [
                jnp.dot(high[:, at : at + pair], ones, preferred_element_type=f32)
                + jnp.dot(low[:, at : at + pair], ones, preferred_element_type=f32)
                for at in range(0, width, pair)
            ],
            axis=1,
        )

    queries = q_ref[...].astype(f32)
    own_scores = head_sums(queries * k_ref[...].astype(f32)) * factor
    new_values = v_ref[...].astype(f32)
    for r in range(block):
        scores[r * ctx_len : (r + 1) * ctx_len, :] = (
            kv[r, :, 0, :].astype(f32) * queries[r : r + 1, :]
        )
    scores[...] = head_sums(scores[...]) * factor
    position = lax.broadcasted_iota(jnp.int32, (ctx_len, width), 0)
    rows = []
    for r in range(block):
        valid = position < lens[step * block + r]
        own = own_scores[r : r + 1, :]
        masked = jnp.where(valid, scores[r * ctx_len : (r + 1) * ctx_len, :], -jnp.inf)
        top = jnp.maximum(jnp.max(masked, axis=0, keepdims=True), own)
        expos = jnp.exp(masked - top)
        own_expo = jnp.exp(own - top)
        total = jnp.sum(expos, axis=0, keepdims=True) + own_expo
        inverse = 1.0 / total
        weights = (expos * inverse).astype(bf16).astype(f32)
        own_weight = (own_expo * inverse).astype(bf16).astype(f32)
        mixed = jnp.sum(weights * kv[r, :, 1, :].astype(f32), axis=0, keepdims=True)
        rows.append(mixed + own_weight * new_values[r : r + 1, :])
    attended[pl.ds(pl.multiple_of(step * block, block), block), :] = jnp.concatenate(rows, axis=0)

    @pl.when(step == pl.num_programs(0) - 1)
    def _():
        load.wait()
        out[...] = jnp.dot(attended[...].astype(bf16), proj[...], preferred_element_type=f32)


def attend(fresh_qkv, kv_cache, cache_len, out_proj):
    tokens, ctx_len, _, width = kv_cache.shape
    block = 8
    fresh = pl.BlockSpec((block, width), lambda i: (i, 0))
    model = out_proj.shape[1]
    return pl.pallas_call(
        functools.partial(attend_kernel, ctx_len),
        grid=(tokens // block,),
        out_shape=jax.ShapeDtypeStruct((tokens, model), jnp.float32),
        in_specs=[
            pl.BlockSpec(memory_space=pltpu.SMEM),
            fresh,
            fresh,
            fresh,
            pl.BlockSpec((block, ctx_len, 2, width), lambda i: (i, 0, 0, 0)),
            pl.BlockSpec(memory_space=pl.ANY),
        ],
        out_specs=pl.BlockSpec((tokens, model), lambda i: (0, 0)),
        scratch_shapes=[
            pltpu.VMEM(out_proj.shape, jnp.bfloat16),
            pltpu.VMEM((tokens, width), jnp.float32),
            pltpu.VMEM((block * ctx_len, width), jnp.float32),
            pltpu.SemaphoreType.DMA,
        ],
        compiler_params=pltpu.CompilerParams(vmem_limit_bytes=40 * 1024 * 1024),
    )(cache_len, fresh_qkv[:, 0], fresh_qkv[:, 1], fresh_qkv[:, 2], kv_cache, out_proj)


def moe_kernel(
    deep,
    plane,
    cores,
    partial,
    residual,
    gain,
    router,
    named,
    gate_hbm,
    up_hbm,
    down_hbm,
    out,
    parts,
    hidden,
    normed,
    gathered,
    gate_w,
    up_w,
    down_w,
    core_out,
    core_in,
    plane_out,
    plane_in,
    deep_out,
    deep_in,
    load_sem,
    parts_send,
    parts_recv,
    own_send,
    pass_send,
    slot_recv,
    cross_send,
    cross_recv,
    core_send,
    core_recv,
    plane_send,
    plane_recv,
    deep_send,
    deep_recv,
):
    me = lax.axis_index("req")
    core = lax.axis_index("tp")
    level = me // plane
    place = lax.rem(me, plane)
    tokens, width = residual.shape
    cols = width // cores
    f32, bf16 = jnp.float32, jnp.bfloat16

    loads = [
        pltpu.make_async_copy(src, dst, load_sem.at[i])
        for i, (src, dst) in enumerate(((gate_hbm, gate_w), (up_hbm, up_w), (down_hbm, down_w)))
    ]
    for load in loads:
        load.start()

    def core_at(i):
        return lax.rem(core + i, cores)

    def level_at(i):
        return lax.rem(level + i, deep)

    def place_at(i):
        return lax.rem(place + i, plane)

    barrier = pltpu.get_barrier_semaphore()
    greeted = [(me, core_at(i)) for i in range(1, cores)]
    greeted += [(level_at(i) * plane + place, core) for i in range(1, deep)]
    greeted += [(level * plane + place_at(i), core) for i in range(1, plane)]
    for device in greeted:
        pl.semaphore_signal(barrier, inc=1, device_id=device, device_id_type=pl.DeviceIdType.MESH)
    pl.semaphore_wait(barrier, len(greeted))

    def send(src, dst, send_sem, recv_sem, device):
        copy = pltpu.make_async_remote_copy(
            src_ref=src,
            dst_ref=dst,
            send_sem=send_sem,
            recv_sem=recv_sem,
            device_id=device,
            device_id_type=pl.DeviceIdType.MESH,
        )
        copy.start()
        started.append(copy)

    def arrived(dst, recv_sem):
        pltpu.make_async_copy(dst, dst, recv_sem).wait()

    started = []
    for i in range(1, cores):
        send(partial, parts.at[i - 1], parts_send.at[i - 1], parts_recv.at[i - 1], (me, core_at(i)))
    for i in range(1, cores):
        arrived(parts.at[i - 1], parts_recv.at[i - 1])
    summed = partial[...]
    for i in range(1, cores):
        summed = summed + parts[i - 1]
    hidden[...] = (residual[...].astype(f32) + summed).astype(bf16)
    values = hidden[...].astype(f32)
    scale_inv = lax.rsqrt(jnp.mean(values * values, axis=-1, keepdims=True) + 1e-05)
    normed[...] = (values * scale_inv * gain[...]).astype(bf16)
    logits = jnp.dot(
        normed[...].astype(f32),
        router[...],
        precision=lax.Precision.HIGHEST,
        preferred_element_type=f32,
    )
    half = router.shape[1] // 2
    lane = lax.broadcasted_iota(jnp.int32, logits.shape, 1)
    chosen = named[...] > 0.0
    top = jnp.max(jnp.where(chosen, logits, -jnp.inf), axis=1, keepdims=True)
    expos = jnp.where(chosen, jnp.exp(jnp.where(chosen, logits, top) - top), 0.0)
    total = jnp.sum(jnp.where(lane < half, expos, 0.0), axis=1, keepdims=True)
    gates = expos / total
    high = gates.astype(bf16).astype(f32)
    own_cols = pl.ds(pl.multiple_of(core * cols, 128), cols)
    gathered[core, me, :, 0:cols] = normed[:, own_cols]
    gathered[core, me, :, cols:] = jnp.where(lane < half, high, gates - high).astype(bf16)

    def spread(k):
        slot = level_at(deep - k) * plane + place if k else me
        block = gathered.at[core, slot]
        for j in range(1, plane):
            send(
                block,
                block,
                pass_send.at[k, j - 1],
                slot_recv.at[slot],
                (level * plane + place_at(j), core),
            )

    def cross(k, j):
        slot = level_at(deep - k) * plane + place_at(j)
        block = gathered.at[core, slot]
        for i in range(1, cores):
            send(
                block,
                block,
                cross_send.at[k, j, i - 1],
                cross_recv.at[i - 1, slot],
                (me, core_at(i)),
            )

    mine = gathered.at[core, me]
    for i in range(1, deep):
        send(mine, mine, own_send.at[i - 1], slot_recv.at[me], (level_at(i) * plane + place, core))
    spread(0)
    cross(0, 0)
    for k in range(1, deep):
        slot = level_at(deep - k) * plane + place
        arrived(gathered.at[core, slot], slot_recv.at[slot])
        spread(k)
        cross(k, 0)

    def collect(k):
        first = level_at(deep - k) * plane
        for j in range(1, plane):
            slot = first + place_at(j)
            arrived(gathered.at[core, slot], slot_recv.at[slot])
            cross(k, j)
        for i in range(1, cores):
            for j in range(plane):
                slot = first + place_at(j)
                arrived(gathered.at[core_at(cores - i), slot], cross_recv.at[i - 1, slot])

    def work(k):
        slots = pl.ds(level_at(deep - k) * plane, plane)
        gate_part = up_part = 0.0
        for t in range(cores):
            block = gathered[t, slots, :, 0:cols].reshape(plane * tokens, cols)
            span = slice(t * cols, (t + 1) * cols)
            gate_part += jnp.dot(block, gate_w[span, :], preferred_element_type=f32)
            up_part += jnp.dot(block, up_w[span, :], preferred_element_type=f32)
        inner = (gate_part * (1.0 / (1.0 + jnp.exp(-gate_part))) * up_part).astype(bf16)
        extra = gathered[0, slots, :, cols:].reshape(plane * tokens, 2 * half).astype(f32)
        spot = lax.broadcasted_iota(jnp.int32, extra.shape, 1)
        weight = jnp.sum(
            jnp.where((spot == me) | (spot == me + half), extra, 0.0), axis=1, keepdims=True
        )
        for i in range(1, cores + 1):
            span = pl.ds(pl.multiple_of(core_at(i) * cols, 128), cols)
            result = jnp.dot(inner, down_w[:, span], preferred_element_type=f32) * weight
            core_out[k, i - 1] = result.astype(core_out.dtype).reshape(plane, tokens, cols)
            if i < cores:
                send(
                    core_out.at[k, i - 1],
                    core_in.at[k, i - 1],
                    core_send.at[k, i - 1],
                    core_recv.at[k, i - 1],
                    (me, core_at(i)),
                )

    def over_plane(k):
        for i in range(1, cores):
            arrived(core_in.at[k, i - 1], core_recv.at[k, i - 1])
        for j in list(range(1, plane)) + [0]:
            whole = core_out[k, cores - 1, place_at(j)].astype(f32)
            for i in range(1, cores):
                whole = whole + core_in[k, i - 1, place_at(j)].astype(f32)
            plane_out[k, j] = whole.astype(bf16)
            if j:
                send(
                    plane_out.at[k, j],
                    plane_in.at[k, j - 1],
                    plane_send.at[k, j - 1],
                    plane_recv.at[k, j - 1],
                    (level * plane + place_at(j), core),
                )

    def over_deep(k):
        whole = plane_out[k, 0].astype(f32)
        for j in range(1, plane):
            arrived(plane_in.at[k, j - 1], plane_recv.at[k, j - 1])
            whole = whole + plane_in[k, j - 1].astype(f32)
        if k:
            deep_out[k - 1] = whole.astype(bf16)
            send(
                deep_out.at[k - 1],
                deep_in.at[k - 1],
                deep_send.at[k - 1],
                deep_recv.at[k - 1],
                (level_at(deep - k) * plane + place, core),
            )
        return whole

    own_sum = None
    for step in range(deep + 2):
        if step < deep:
            collect(step)
            if step == 0:
                for load in loads:
                    load.wait()
            work(step)
        if 1 <= step <= deep:
            over_plane(step - 1)
        if step >= 2:
            found = over_deep(step - 2)
            own_sum = found if step == 2 else own_sum
    for k in range(1, deep):
        arrived(deep_in.at[k - 1], deep_recv.at[k - 1])
        own_sum = own_sum + deep_in[k - 1].astype(f32)
    out[...] = (hidden[:, own_cols].astype(f32) + own_sum).astype(bf16)
    for copy in started:
        copy.wait_send()


def moe_call(partial, residual, gain, router, named, gate_w, up_w, down_w):
    shards, cores = lax.axis_size("req"), lax.axis_size("tp")
    deep = 4
    plane = shards // deep
    tokens, width = residual.shape
    units = down_w.shape[0]
    cols = width // cores
    bf16, dma = jnp.bfloat16, pltpu.SemaphoreType.DMA
    others = cores - 1
    vmem = pl.BlockSpec(memory_space=pltpu.VMEM)
    hbm = pl.BlockSpec(memory_space=pl.ANY)
    return pl.pallas_call(
        functools.partial(moe_kernel, deep, plane, cores),
        out_shape=jax.ShapeDtypeStruct((tokens, cols), bf16),
        in_specs=[vmem] * 5 + [hbm] * 3,
        out_specs=vmem,
        scratch_shapes=[
            pltpu.VMEM((others, tokens, width), jnp.float32),
            pltpu.VMEM((tokens, width), bf16),
            pltpu.VMEM((tokens, width), bf16),
            pltpu.VMEM((cores, shards, tokens, cols + router.shape[1]), bf16),
            pltpu.VMEM((width, units), bf16),
            pltpu.VMEM((width, units), bf16),
            pltpu.VMEM((units, width), bf16),
            pltpu.VMEM((deep, cores, plane, tokens, cols), bf16),
            pltpu.VMEM((deep, others, plane, tokens, cols), bf16),
            pltpu.VMEM((deep, plane, tokens, cols), bf16),
            pltpu.VMEM((deep, plane - 1, tokens, cols), bf16),
            pltpu.VMEM((deep - 1, tokens, cols), bf16),
            pltpu.VMEM((deep - 1, tokens, cols), bf16),
            dma((3,)),
            dma((others,)),
            dma((others,)),
            dma((deep - 1,)),
            dma((deep, plane - 1)),
            dma((shards,)),
            dma((deep, plane, others)),
            dma((others, shards)),
            dma((deep, others)),
            dma((deep, others)),
            dma((deep, plane - 1)),
            dma((deep, plane - 1)),
            dma((deep - 1,)),
            dma((deep - 1,)),
        ],
        compiler_params=pltpu.CompilerParams(
            collective_id=0, has_side_effects=True, vmem_limit_bytes=56 * 1024 * 1024
        ),
    )(partial, residual, gain, router, named, gate_w, up_w, down_w)


def local(
    residual,
    fresh_qkv,
    kv_cache,
    cache_len,
    out_proj,
    norm_gain,
    router_weight,
    expert_ids,
    gate_up,
    down_proj,
):
    experts = lax.axis_size("req")
    partial_value = attend(fresh_qkv, kv_cache, cache_len, out_proj)
    half = 64 * (-(-experts // 64))
    lanes = lax.rem(jnp.arange(2 * half, dtype=jnp.int32), half)
    named = jnp.any(expert_ids[:, :, None] == lanes[None, None, :], axis=1).astype(jnp.float32)
    router = jnp.pad(router_weight, ((0, 0), (0, half - experts)))
    router = jnp.concatenate([router, router], axis=1)
    return moe_call(
        partial_value,
        residual,
        norm_gain[None, :],
        router,
        named,
        gate_up[0, :, 0],
        gate_up[0, :, 1],
        down_proj[0],
    )


def solution(mesh):
    in_specs = (
        P("req", None),
        P("req", None, "tp"),
        P("req", None, None, "tp"),
        P("req"),
        P("tp", None),
        P(),
        P(),
        P("req", None),
        P("req", None, None, "tp"),
        P("req", "tp", None),
    )
    out_specs = P("req", "tp")
    return jax.shard_map(local, mesh=mesh, in_specs=in_specs, out_specs=out_specs, check_vma=False)
```

```python
import functools

import jax
import jax.numpy as jnp
from jax import lax
from jax.experimental import pallas as pl
from jax.experimental.pallas import tpu as pltpu
from jax.sharding import PartitionSpec as P

HD = 128


def attend_kernel(ctx_len, lens, q_ref, k_ref, v_ref, kv, proj_hbm, out, proj, attended, scores, load_sem):
    step = pl.program_id(0)
    load = pltpu.make_async_copy(proj_hbm, proj, load_sem)

    @pl.when(step == 0)
    def _():
        load.start()

    f32, bf16 = jnp.float32, jnp.bfloat16
    block, width = q_ref.shape
    pair = 2 * HD
    row = lax.broadcasted_iota(jnp.int32, (pair, pair), 0) // HD
    column = lax.broadcasted_iota(jnp.int32, (pair, pair), 1) // HD
    ones = jnp.where(row == column, 1.0, 0.0).astype(bf16)
    factor = HD ** (-0.5)

    def head_sums(product):
        high = product.astype(bf16)
        low = (product - high.astype(f32)).astype(bf16)
        return jnp.concatenate(
            [
                jnp.dot(high[:, at : at + pair], ones, preferred_element_type=f32)
                + jnp.dot(low[:, at : at + pair], ones, preferred_element_type=f32)
                for at in range(0, width, pair)
            ],
            axis=1,
        )

    queries = q_ref[...].astype(f32)
    own_scores = head_sums(queries * k_ref[...].astype(f32)) * factor
    new_values = v_ref[...].astype(f32)
    for r in range(block):
        scores[r * ctx_len : (r + 1) * ctx_len, :] = (
            kv[r, :, 0, :].astype(f32) * queries[r : r + 1, :]
        )
    scores[...] = head_sums(scores[...]) * factor
    position = lax.broadcasted_iota(jnp.int32, (ctx_len, width), 0)
    rows = []
    for r in range(block):
        valid = position < lens[step * block + r]
        own = own_scores[r : r + 1, :]
        masked = jnp.where(valid, scores[r * ctx_len : (r + 1) * ctx_len, :], -jnp.inf)
        top = jnp.maximum(jnp.max(masked, axis=0, keepdims=True), own)
        expos = jnp.exp(masked - top)
        own_expo = jnp.exp(own - top)
        total = jnp.sum(expos, axis=0, keepdims=True) + own_expo
        inverse = 1.0 / total
        weights = (expos * inverse).astype(bf16).astype(f32)
        own_weight = (own_expo * inverse).astype(bf16).astype(f32)
        mixed = jnp.sum(weights * kv[r, :, 1, :].astype(f32), axis=0, keepdims=True)
        rows.append(mixed + own_weight * new_values[r : r + 1, :])
    attended[pl.ds(pl.multiple_of(step * block, block), block), :] = jnp.concatenate(rows, axis=0)

    @pl.when(step == pl.num_programs(0) - 1)
    def _():
        load.wait()
        out[...] = jnp.dot(attended[...].astype(bf16), proj[...], preferred_element_type=f32)


def attend(fresh_qkv, kv_cache, cache_len, out_proj):
    tokens, ctx_len, _, width = kv_cache.shape
    block = 8
    fresh = pl.BlockSpec((block, width), lambda i: (i, 0))
    model = out_proj.shape[1]
    return pl.pallas_call(
        functools.partial(attend_kernel, ctx_len),
        grid=(tokens // block,),
        out_shape=jax.ShapeDtypeStruct((tokens, model), jnp.float32),
        in_specs=[
            pl.BlockSpec(memory_space=pltpu.SMEM),
            fresh,
            fresh,
            fresh,
            pl.BlockSpec((block, ctx_len, 2, width), lambda i: (i, 0, 0, 0)),
            pl.BlockSpec(memory_space=pl.ANY),
        ],
        out_specs=pl.BlockSpec((tokens, model), lambda i: (0, 0)),
        scratch_shapes=[
            pltpu.VMEM(out_proj.shape, jnp.bfloat16),
            pltpu.VMEM((tokens, width), jnp.float32),
            pltpu.VMEM((block * ctx_len, width), jnp.float32),
            pltpu.SemaphoreType.DMA,
        ],
        compiler_params=pltpu.CompilerParams(vmem_limit_bytes=60 * 1024 * 1024),
    )(cache_len, fresh_qkv[:, 0], fresh_qkv[:, 1], fresh_qkv[:, 2], kv_cache, out_proj)


def moe_kernel(
    deep,
    plane,
    cores,
    partial,
    residual,
    gain,
    router,
    ids,
    both_hbm,
    down_hbm,
    out,
    parts,
    hidden,
    normed,
    gathered,
    both_w,
    gate_w,
    up_w,
    down_w,
    core_out,
    core_in,
    plane_out,
    plane_in,
    deep_out,
    deep_in,
    load_sem,
    parts_send,
    parts_recv,
    own_send,
    pass_send,
    slot_recv,
    cross_send,
    cross_recv,
    core_send,
    core_recv,
    plane_send,
    plane_recv,
    deep_send,
    deep_recv,
):
    me = lax.axis_index("req")
    core = lax.axis_index("tp")
    level = me // plane
    place = lax.rem(me, plane)
    tokens, width = residual.shape
    cols = width // cores
    f32, bf16 = jnp.float32, jnp.bfloat16

    loads = [
        pltpu.make_async_copy(src, dst, load_sem.at[i])
        for i, (src, dst) in enumerate(((both_hbm, both_w), (down_hbm, down_w)))
    ]
    for load in loads:
        load.start()

    def core_at(i):
        return lax.rem(core + i, cores)

    def level_at(i):
        return lax.rem(level + i, deep)

    def place_at(i):
        return lax.rem(place + i, plane)

    barrier = pltpu.get_barrier_semaphore()
    greeted = [(me, core_at(i)) for i in range(1, cores)]
    greeted += [(level_at(i) * plane + place, core) for i in range(1, deep)]
    greeted += [(level * plane + place_at(i), core) for i in range(1, plane)]
    for device in greeted:
        pl.semaphore_signal(barrier, inc=1, device_id=device, device_id_type=pl.DeviceIdType.MESH)
    pl.semaphore_wait(barrier, len(greeted))

    def send(src, dst, send_sem, recv_sem, device):
        copy = pltpu.make_async_remote_copy(
            src_ref=src,
            dst_ref=dst,
            send_sem=send_sem,
            recv_sem=recv_sem,
            device_id=device,
            device_id_type=pl.DeviceIdType.MESH,
        )
        copy.start()
        started.append(copy)

    def arrived(dst, recv_sem):
        pltpu.make_async_copy(dst, dst, recv_sem).wait()

    started = []
    for i in range(1, cores):
        send(partial, parts.at[i - 1], parts_send.at[i - 1], parts_recv.at[i - 1], (me, core_at(i)))
    for i in range(1, cores):
        arrived(parts.at[i - 1], parts_recv.at[i - 1])
    summed = partial[...]
    for i in range(1, cores):
        summed = summed + parts[i - 1]
    hidden[...] = (residual[...].astype(f32) + summed).astype(bf16)
    values = hidden[...].astype(f32)
    scale_inv = lax.rsqrt(jnp.mean(values * values, axis=-1, keepdims=True) + 1e-05)
    normed[...] = (values * scale_inv * gain[...]).astype(bf16)
    logits = jnp.dot(
        normed[...].astype(f32),
        router[...],
        precision=lax.Precision.HIGHEST,
        preferred_element_type=f32,
    )
    experts = router.shape[1]
    half = 64 * (-(-experts // 64))
    source = lax.broadcasted_iota(jnp.int32, (experts, 2 * half), 0)
    target = lax.rem(lax.broadcasted_iota(jnp.int32, (experts, 2 * half), 1), half)
    logits = jnp.dot(
        logits,
        jnp.where(source == target, 1.0, 0.0).astype(f32),
        precision=lax.Precision.HIGHEST,
        preferred_element_type=f32,
    )
    lane = lax.broadcasted_iota(jnp.int32, logits.shape, 1)
    lane_expert = lax.rem(lane, half)
    chosen = ids[:, 0:1] == lane_expert
    for k in range(1, ids.shape[1]):
        chosen = chosen | (ids[:, k : k + 1] == lane_expert)
    top = jnp.max(jnp.where(chosen, logits, -jnp.inf), axis=1, keepdims=True)
    expos = jnp.where(chosen, jnp.exp(jnp.where(chosen, logits, top) - top), 0.0)
    total = jnp.sum(jnp.where(lane < half, expos, 0.0), axis=1, keepdims=True)
    gates = expos / total
    high = gates.astype(bf16).astype(f32)
    own_cols = pl.ds(pl.multiple_of(core * cols, 128), cols)
    gathered[core, me, :, 0:cols] = normed[:, own_cols]
    gathered[core, me, :, cols:] = jnp.where(lane < half, high, gates - high).astype(bf16)

    def spread(k):
        slot = level_at(deep - k) * plane + place if k else me
        block = gathered.at[core, slot]
        for j in range(1, plane):
            send(
                block,
                block,
                pass_send.at[k, j - 1],
                slot_recv.at[slot],
                (level * plane + place_at(j), core),
            )

    def cross(k, j):
        slot = level_at(deep - k) * plane + place_at(j)
        block = gathered.at[core, slot]
        for i in range(1, cores):
            send(
                block,
                block,
                cross_send.at[k, j, i - 1],
                cross_recv.at[i - 1, slot],
                (me, core_at(i)),
            )

    mine = gathered.at[core, me]
    for i in range(1, deep):
        send(mine, mine, own_send.at[i - 1], slot_recv.at[me], (level_at(i) * plane + place, core))
    spread(0)
    cross(0, 0)
    loads[0].wait()

    def split(k):
        rows = 128
        quarter = width // deep

        def one(i, carry):
            span = pl.ds(pl.multiple_of(k * quarter + i * rows, rows), rows)
            gate_w[span, :] = both_w[span, 0, :]
            up_w[span, :] = both_w[span, 1, :]
            return carry

        lax.fori_loop(0, quarter // rows, one, 0)

    split(0)
    for k in range(1, deep):
        slot = level_at(deep - k) * plane + place
        arrived(gathered.at[core, slot], slot_recv.at[slot])
        spread(k)
        cross(k, 0)
        split(k)

    def collect(k):
        first = level_at(deep - k) * plane
        for j in range(1, plane):
            slot = first + place_at(j)
            arrived(gathered.at[core, slot], slot_recv.at[slot])
            cross(k, j)
        for i in range(1, cores):
            for j in range(plane):
                slot = first + place_at(j)
                arrived(gathered.at[core_at(cores - i), slot], cross_recv.at[i - 1, slot])

    def work(k):
        slots = pl.ds(level_at(deep - k) * plane, plane)
        gate_part = up_part = 0.0
        for t in range(cores):
            block = gathered[t, slots, :, 0:cols].reshape(plane * tokens, cols)
            span = slice(t * cols, (t + 1) * cols)
            gate_part += jnp.dot(block, gate_w[span, :], preferred_element_type=f32)
            up_part += jnp.dot(block, up_w[span, :], preferred_element_type=f32)
        inner = (gate_part * (1.0 / (1.0 + jnp.exp(-gate_part))) * up_part).astype(bf16)
        extra = gathered[0, slots, :, cols:].reshape(plane * tokens, 2 * half).astype(f32)
        spot = lax.broadcasted_iota(jnp.int32, extra.shape, 1)
        weight = jnp.sum(
            jnp.where((spot == me) | (spot == me + half), extra, 0.0), axis=1, keepdims=True
        )
        for i in range(1, cores + 1):
            span = pl.ds(pl.multiple_of(core_at(i) * cols, 128), cols)
            result = jnp.dot(inner, down_w[:, span], preferred_element_type=f32) * weight
            core_out[k, i - 1] = result.astype(core_out.dtype).reshape(plane, tokens, cols)
            if i < cores:
                send(
                    core_out.at[k, i - 1],
                    core_in.at[k, i - 1],
                    core_send.at[k, i - 1],
                    core_recv.at[k, i - 1],
                    (me, core_at(i)),
                )

    def over_plane(k):
        for i in range(1, cores):
            arrived(core_in.at[k, i - 1], core_recv.at[k, i - 1])
        for j in list(range(1, plane)) + [0]:
            whole = core_out[k, cores - 1, place_at(j)].astype(f32)
            for i in range(1, cores):
                whole = whole + core_in[k, i - 1, place_at(j)].astype(f32)
            plane_out[k, j] = whole.astype(bf16)
            if j:
                send(
                    plane_out.at[k, j],
                    plane_in.at[k, j - 1],
                    plane_send.at[k, j - 1],
                    plane_recv.at[k, j - 1],
                    (level * plane + place_at(j), core),
                )

    def over_deep(k):
        whole = plane_out[k, 0].astype(f32)
        for j in range(1, plane):
            arrived(plane_in.at[k, j - 1], plane_recv.at[k, j - 1])
            whole = whole + plane_in[k, j - 1].astype(f32)
        if k:
            deep_out[k - 1] = whole.astype(bf16)
            send(
                deep_out.at[k - 1],
                deep_in.at[k - 1],
                deep_send.at[k - 1],
                deep_recv.at[k - 1],
                (level_at(deep - k) * plane + place, core),
            )
        return whole

    own_sum = None
    for step in range(deep + 2):
        if step < deep:
            collect(step)
            if step == 0:
                loads[1].wait()
            work(step)
        if 1 <= step <= deep:
            over_plane(step - 1)
        if step >= 2:
            found = over_deep(step - 2)
            own_sum = found if step == 2 else own_sum
    for k in range(1, deep):
        arrived(deep_in.at[k - 1], deep_recv.at[k - 1])
        own_sum = own_sum + deep_in[k - 1].astype(f32)
    out[...] = (hidden[:, own_cols].astype(f32) + own_sum).astype(bf16)
    for copy in started:
        copy.wait_send()


def moe_call(partial, residual, gain, router, ids, both_w, down_w):
    shards, cores = lax.axis_size("req"), lax.axis_size("tp")
    deep = 4
    plane = shards // deep
    tokens, width = residual.shape
    units = down_w.shape[0]
    cols = width // cores
    bf16, dma = jnp.bfloat16, pltpu.SemaphoreType.DMA
    others = cores - 1
    vmem = pl.BlockSpec(memory_space=pltpu.VMEM)
    hbm = pl.BlockSpec(memory_space=pl.ANY)
    return pl.pallas_call(
        functools.partial(moe_kernel, deep, plane, cores),
        out_shape=jax.ShapeDtypeStruct((tokens, cols), bf16),
        in_specs=[vmem] * 5 + [hbm] * 2,
        out_specs=vmem,
        scratch_shapes=[
            pltpu.VMEM((others, tokens, width), jnp.float32),
            pltpu.VMEM((tokens, width), bf16),
            pltpu.VMEM((tokens, width), bf16),
            pltpu.VMEM((cores, shards, tokens, cols + 128 * (-(-shards // 64))), bf16),
            pltpu.VMEM((width, 2, units), bf16),
            pltpu.VMEM((width, units), bf16),
            pltpu.VMEM((width, units), bf16),
            pltpu.VMEM((units, width), bf16),
            pltpu.VMEM((deep, cores, plane, tokens, cols), bf16),
            pltpu.VMEM((deep, others, plane, tokens, cols), bf16),
            pltpu.VMEM((deep, plane, tokens, cols), bf16),
            pltpu.VMEM((deep, plane - 1, tokens, cols), bf16),
            pltpu.VMEM((deep - 1, tokens, cols), bf16),
            pltpu.VMEM((deep - 1, tokens, cols), bf16),
            dma((2,)),
            dma((others,)),
            dma((others,)),
            dma((deep - 1,)),
            dma((deep, plane - 1)),
            dma((shards,)),
            dma((deep, plane, others)),
            dma((others, shards)),
            dma((deep, others)),
            dma((deep, others)),
            dma((deep, plane - 1)),
            dma((deep, plane - 1)),
            dma((deep - 1,)),
            dma((deep - 1,)),
        ],
        compiler_params=pltpu.CompilerParams(
            collective_id=0, has_side_effects=True, vmem_limit_bytes=56 * 1024 * 1024
        ),
    )(partial, residual, gain, router, ids, both_w, down_w)


def local(
    residual,
    fresh_qkv,
    kv_cache,
    cache_len,
    out_proj,
    norm_gain,
    router_weight,
    expert_ids,
    gate_up,
    down_proj,
):
    partial_value = attend(fresh_qkv, kv_cache, cache_len, out_proj)
    return moe_call(
        partial_value,
        residual,
        norm_gain[None, :],
        router_weight,
        expert_ids,
        gate_up[0],
        down_proj[0],
    )


def solution(mesh):
    in_specs = (
        P("req", None),
        P("req", None, "tp"),
        P("req", None, None, "tp"),
        P("req"),
        P("tp", None),
        P(),
        P(),
        P("req", None),
        P("req", None, None, "tp"),
        P("req", "tp", None),
    )
    out_specs = P("req", "tp")
    return jax.shard_map(local, mesh=mesh, in_specs=in_specs, out_specs=out_specs, check_vma=False)
```

```python
import functools

import jax
import jax.numpy as jnp
from jax import lax
from jax.experimental import pallas as pl
from jax.experimental.pallas import tpu as pltpu
from jax.sharding import PartitionSpec as P

HD = 128


def attend_kernel(ctx_len, lens, q_ref, k_ref, v_ref, kv, proj_hbm, out, proj, attended, scores, load_sem):
    step = pl.program_id(0)
    load = pltpu.make_async_copy(proj_hbm, proj, load_sem)

    @pl.when(step == 0)
    def _():
        load.start()

    f32, bf16 = jnp.float32, jnp.bfloat16
    block, width = q_ref.shape
    pair = 2 * HD
    row = lax.broadcasted_iota(jnp.int32, (pair, pair), 0) // HD
    column = lax.broadcasted_iota(jnp.int32, (pair, pair), 1) // HD
    ones = jnp.where(row == column, 1.0, 0.0).astype(bf16)
    factor = HD ** (-0.5)

    def head_sums(product):
        high = product.astype(bf16)
        low = (product - high.astype(f32)).astype(bf16)
        return jnp.concatenate(
            [
                jnp.dot(high[:, at : at + pair], ones, preferred_element_type=f32)
                + jnp.dot(low[:, at : at + pair], ones, preferred_element_type=f32)
                for at in range(0, width, pair)
            ],
            axis=1,
        )

    queries = q_ref[...].astype(f32)
    own_scores = head_sums(queries * k_ref[...].astype(f32)) * factor
    new_values = v_ref[...].astype(f32)
    for r in range(block):
        scores[r * ctx_len : (r + 1) * ctx_len, :] = (
            kv[r, :, 0, :].astype(f32) * queries[r : r + 1, :]
        )
    scores[...] = head_sums(scores[...]) * factor
    position = lax.broadcasted_iota(jnp.int32, (ctx_len, width), 0)
    rows = []
    for r in range(block):
        valid = position < lens[step * block + r]
        own = own_scores[r : r + 1, :]
        masked = jnp.where(valid, scores[r * ctx_len : (r + 1) * ctx_len, :], -jnp.inf)
        top = jnp.maximum(jnp.max(masked, axis=0, keepdims=True), own)
        expos = jnp.exp(masked - top)
        own_expo = jnp.exp(own - top)
        total = jnp.sum(expos, axis=0, keepdims=True) + own_expo
        inverse = 1.0 / total
        weights = (expos * inverse).astype(bf16).astype(f32)
        own_weight = (own_expo * inverse).astype(bf16).astype(f32)
        mixed = jnp.sum(weights * kv[r, :, 1, :].astype(f32), axis=0, keepdims=True)
        rows.append(mixed + own_weight * new_values[r : r + 1, :])
    attended[pl.ds(pl.multiple_of(step * block, block), block), :] = jnp.concatenate(rows, axis=0)

    @pl.when(step == pl.num_programs(0) - 1)
    def _():
        load.wait()
        out[...] = jnp.dot(attended[...].astype(bf16), proj[...], preferred_element_type=f32)


def attend(fresh_qkv, kv_cache, cache_len, out_proj):
    tokens, ctx_len, _, width = kv_cache.shape
    block = 8
    fresh = pl.BlockSpec((block, width), lambda i: (i, 0))
    model = out_proj.shape[1]
    return pl.pallas_call(
        functools.partial(attend_kernel, ctx_len),
        grid=(tokens // block,),
        out_shape=jax.ShapeDtypeStruct((tokens, model), jnp.float32),
        in_specs=[
            pl.BlockSpec(memory_space=pltpu.SMEM),
            fresh,
            fresh,
            fresh,
            pl.BlockSpec((block, ctx_len, 2, width), lambda i: (i, 0, 0, 0)),
            pl.BlockSpec(memory_space=pl.ANY),
        ],
        out_specs=pl.BlockSpec((tokens, model), lambda i: (0, 0)),
        scratch_shapes=[
            pltpu.VMEM(out_proj.shape, jnp.bfloat16),
            pltpu.VMEM((tokens, width), jnp.float32),
            pltpu.VMEM((block * ctx_len, width), jnp.float32),
            pltpu.SemaphoreType.DMA,
        ],
        compiler_params=pltpu.CompilerParams(vmem_limit_bytes=60 * 1024 * 1024),
    )(cache_len, fresh_qkv[:, 0], fresh_qkv[:, 1], fresh_qkv[:, 2], kv_cache, out_proj)


def moe_kernel(
    deep,
    plane,
    cores,
    partial,
    residual,
    gain,
    router,
    ids,
    both_hbm,
    down_hbm,
    out,
    parts,
    hidden,
    normed,
    gathered,
    both_w,
    gate_w,
    up_w,
    down_w,
    core_out,
    core_in,
    plane_out,
    plane_in,
    deep_out,
    deep_in,
    load_sem,
    parts_send,
    parts_recv,
    own_send,
    pass_send,
    slot_recv,
    cross_send,
    cross_recv,
    core_send,
    core_recv,
    plane_send,
    plane_recv,
    deep_send,
    deep_recv,
):
    me = lax.axis_index("req")
    core = lax.axis_index("tp")
    level = me // plane
    place = lax.rem(me, plane)
    tokens, width = residual.shape
    cols = width // cores
    f32, bf16 = jnp.float32, jnp.bfloat16

    loads = [
        pltpu.make_async_copy(src, dst, load_sem.at[i])
        for i, (src, dst) in enumerate(((both_hbm, both_w), (down_hbm, down_w)))
    ]
    for load in loads:
        load.start()

    def core_at(i):
        return lax.rem(core + i, cores)

    def level_at(i):
        return lax.rem(level + i, deep)

    def place_at(i):
        return lax.rem(place + i, plane)

    barrier = pltpu.get_barrier_semaphore()
    greeted = [(me, core_at(i)) for i in range(1, cores)]
    greeted += [(level_at(i) * plane + place, core) for i in range(1, deep)]
    greeted += [(level * plane + place_at(i), core) for i in range(1, plane)]
    for device in greeted:
        pl.semaphore_signal(barrier, inc=1, device_id=device, device_id_type=pl.DeviceIdType.MESH)
    pl.semaphore_wait(barrier, len(greeted))

    def send(src, dst, send_sem, recv_sem, device):
        copy = pltpu.make_async_remote_copy(
            src_ref=src,
            dst_ref=dst,
            send_sem=send_sem,
            recv_sem=recv_sem,
            device_id=device,
            device_id_type=pl.DeviceIdType.MESH,
        )
        copy.start()
        started.append(copy)

    def arrived(dst, recv_sem):
        pltpu.make_async_copy(dst, dst, recv_sem).wait()

    started = []
    for i in range(1, cores):
        send(partial, parts.at[i - 1], parts_send.at[i - 1], parts_recv.at[i - 1], (me, core_at(i)))
    for i in range(1, cores):
        arrived(parts.at[i - 1], parts_recv.at[i - 1])
    summed = partial[...]
    for i in range(1, cores):
        summed = summed + parts[i - 1]
    hidden[...] = (residual[...].astype(f32) + summed).astype(bf16)
    values = hidden[...].astype(f32)
    scale_inv = lax.rsqrt(jnp.mean(values * values, axis=-1, keepdims=True) + 1e-05)
    normed[...] = (values * scale_inv * gain[...]).astype(bf16)
    logits = lax.dot_general(
        normed[...].astype(f32),
        router[...],
        (((1,), (1,)), ((), ())),
        precision=lax.Precision.HIGHEST,
        preferred_element_type=f32,
    )
    experts = router.shape[0]
    half = 64 * (-(-experts // 64))
    source = lax.broadcasted_iota(jnp.int32, (experts, 2 * half), 0)
    target = lax.rem(lax.broadcasted_iota(jnp.int32, (experts, 2 * half), 1), half)
    lanes = jnp.where(source == target, 1.0, 0.0).astype(f32)
    logits = jnp.dot(logits, lanes, precision=lax.Precision.HIGHEST, preferred_element_type=f32)
    lane = lax.broadcasted_iota(jnp.int32, logits.shape, 1)
    expert = lax.broadcasted_iota(jnp.int32, (experts, tokens), 0)
    named = ids[0:1, :] == expert
    for k in range(1, ids.shape[0]):
        named = named | (ids[k : k + 1, :] == expert)
    named = jnp.where(named, 1.0, 0.0).astype(f32)
    chosen = (
        lax.dot_general(named, lanes, (((0,), (0,)), ((), ())), preferred_element_type=f32) > 0.5
    )
    top = jnp.max(jnp.where(chosen, logits, -jnp.inf), axis=1, keepdims=True)
    expos = jnp.where(chosen, jnp.exp(jnp.where(chosen, logits, top) - top), 0.0)
    total = jnp.sum(jnp.where(lane < half, expos, 0.0), axis=1, keepdims=True)
    gates = expos / total
    high = gates.astype(bf16).astype(f32)
    own_cols = pl.ds(pl.multiple_of(core * cols, 128), cols)
    gathered[core, me, :, 0:cols] = normed[:, own_cols]
    gathered[core, me, :, cols:] = jnp.where(lane < half, high, gates - high).astype(bf16)

    def spread(k):
        slot = level_at(deep - k) * plane + place if k else me
        block = gathered.at[core, slot]
        for j in range(1, plane):
            send(
                block,
                block,
                pass_send.at[k, j - 1],
                slot_recv.at[slot],
                (level * plane + place_at(j), core),
            )

    def cross(k, j):
        slot = level_at(deep - k) * plane + place_at(j)
        block = gathered.at[core, slot]
        for i in range(1, cores):
            send(
                block,
                block,
                cross_send.at[k, j, i - 1],
                cross_recv.at[i - 1, slot],
                (me, core_at(i)),
            )

    mine = gathered.at[core, me]
    for i in range(1, deep):
        send(mine, mine, own_send.at[i - 1], slot_recv.at[me], (level_at(i) * plane + place, core))
    spread(0)
    cross(0, 0)
    loads[0].wait()

    def split(k):
        rows = 128
        quarter = width // deep

        def one(i, carry):
            span = pl.ds(pl.multiple_of(k * quarter + i * rows, rows), rows)
            gate_w[span, :] = both_w[span, 0, :]
            up_w[span, :] = both_w[span, 1, :]
            return carry

        lax.fori_loop(0, quarter // rows, one, 0)

    split(0)
    for k in range(1, deep):
        slot = level_at(deep - k) * plane + place
        arrived(gathered.at[core, slot], slot_recv.at[slot])
        spread(k)
        cross(k, 0)
        split(k)

    def collect(k):
        first = level_at(deep - k) * plane
        for j in range(1, plane):
            slot = first + place_at(j)
            arrived(gathered.at[core, slot], slot_recv.at[slot])
            cross(k, j)
        for i in range(1, cores):
            for j in range(plane):
                slot = first + place_at(j)
                arrived(gathered.at[core_at(cores - i), slot], cross_recv.at[i - 1, slot])

    def work(k):
        slots = pl.ds(level_at(deep - k) * plane, plane)
        gate_part = up_part = 0.0
        for t in range(cores):
            block = gathered[t, slots, :, 0:cols].reshape(plane * tokens, cols)
            span = slice(t * cols, (t + 1) * cols)
            gate_part += jnp.dot(block, gate_w[span, :], preferred_element_type=f32)
            up_part += jnp.dot(block, up_w[span, :], preferred_element_type=f32)
        inner = (gate_part * (1.0 / (1.0 + jnp.exp(-gate_part))) * up_part).astype(bf16)
        extra = gathered[0, slots, :, cols:].reshape(plane * tokens, 2 * half).astype(f32)
        spot = lax.broadcasted_iota(jnp.int32, extra.shape, 1)
        weight = jnp.sum(
            jnp.where((spot == me) | (spot == me + half), extra, 0.0), axis=1, keepdims=True
        )
        for i in range(1, cores + 1):
            span = pl.ds(pl.multiple_of(core_at(i) * cols, 128), cols)
            result = jnp.dot(inner, down_w[:, span], preferred_element_type=f32) * weight
            core_out[k, i - 1] = result.astype(core_out.dtype).reshape(plane, tokens, cols)
            if i < cores:
                send(
                    core_out.at[k, i - 1],
                    core_in.at[k, i - 1],
                    core_send.at[k, i - 1],
                    core_recv.at[k, i - 1],
                    (me, core_at(i)),
                )

    def over_plane(k):
        for i in range(1, cores):
            arrived(core_in.at[k, i - 1], core_recv.at[k, i - 1])
        for j in list(range(1, plane)) + [0]:
            whole = core_out[k, cores - 1, place_at(j)].astype(f32)
            for i in range(1, cores):
                whole = whole + core_in[k, i - 1, place_at(j)].astype(f32)
            plane_out[k, j] = whole.astype(bf16)
            if j:
                send(
                    plane_out.at[k, j],
                    plane_in.at[k, j - 1],
                    plane_send.at[k, j - 1],
                    plane_recv.at[k, j - 1],
                    (level * plane + place_at(j), core),
                )

    def over_deep(k):
        whole = plane_out[k, 0].astype(f32)
        for j in range(1, plane):
            arrived(plane_in.at[k, j - 1], plane_recv.at[k, j - 1])
            whole = whole + plane_in[k, j - 1].astype(f32)
        if k:
            deep_out[k - 1] = whole.astype(bf16)
            send(
                deep_out.at[k - 1],
                deep_in.at[k - 1],
                deep_send.at[k - 1],
                deep_recv.at[k - 1],
                (level_at(deep - k) * plane + place, core),
            )
        return whole

    own_sum = None
    for step in range(deep + 2):
        if step < deep:
            collect(step)
            if step == 0:
                loads[1].wait()
            work(step)
        if 1 <= step <= deep:
            over_plane(step - 1)
        if step >= 2:
            found = over_deep(step - 2)
            own_sum = found if step == 2 else own_sum
    for k in range(1, deep):
        arrived(deep_in.at[k - 1], deep_recv.at[k - 1])
        own_sum = own_sum + deep_in[k - 1].astype(f32)
    out[...] = (hidden[:, own_cols].astype(f32) + own_sum).astype(bf16)
    for copy in started:
        copy.wait_send()


def moe_call(partial, residual, gain, router, ids, both_w, down_w):
    shards, cores = lax.axis_size("req"), lax.axis_size("tp")
    deep = 4
    plane = shards // deep
    tokens, width = residual.shape
    units = down_w.shape[0]
    cols = width // cores
    bf16, dma = jnp.bfloat16, pltpu.SemaphoreType.DMA
    others = cores - 1
    vmem = pl.BlockSpec(memory_space=pltpu.VMEM)
    hbm = pl.BlockSpec(memory_space=pl.ANY)
    return pl.pallas_call(
        functools.partial(moe_kernel, deep, plane, cores),
        out_shape=jax.ShapeDtypeStruct((tokens, cols), bf16),
        in_specs=[vmem] * 5 + [hbm] * 2,
        out_specs=vmem,
        scratch_shapes=[
            pltpu.VMEM((others, tokens, width), jnp.float32),
            pltpu.VMEM((tokens, width), bf16),
            pltpu.VMEM((tokens, width), bf16),
            pltpu.VMEM((cores, shards, tokens, cols + 128 * (-(-shards // 64))), bf16),
            pltpu.VMEM((width, 2, units), bf16),
            pltpu.VMEM((width, units), bf16),
            pltpu.VMEM((width, units), bf16),
            pltpu.VMEM((units, width), bf16),
            pltpu.VMEM((deep, cores, plane, tokens, cols), bf16),
            pltpu.VMEM((deep, others, plane, tokens, cols), bf16),
            pltpu.VMEM((deep, plane, tokens, cols), bf16),
            pltpu.VMEM((deep, plane - 1, tokens, cols), bf16),
            pltpu.VMEM((deep - 1, tokens, cols), bf16),
            pltpu.VMEM((deep - 1, tokens, cols), bf16),
            dma((2,)),
            dma((others,)),
            dma((others,)),
            dma((deep - 1,)),
            dma((deep, plane - 1)),
            dma((shards,)),
            dma((deep, plane, others)),
            dma((others, shards)),
            dma((deep, others)),
            dma((deep, others)),
            dma((deep, plane - 1)),
            dma((deep, plane - 1)),
            dma((deep - 1,)),
            dma((deep - 1,)),
        ],
        compiler_params=pltpu.CompilerParams(
            collective_id=0, has_side_effects=True, vmem_limit_bytes=56 * 1024 * 1024
        ),
    )(partial, residual, gain, router, ids, both_w, down_w)


def local(
    residual,
    fresh_qkv,
    kv_cache,
    cache_len,
    out_proj,
    norm_gain,
    router_weight,
    expert_ids,
    gate_up,
    down_proj,
):
    partial_value = attend(fresh_qkv, kv_cache, cache_len, out_proj)
    return moe_call(
        partial_value,
        residual,
        norm_gain[None, :],
        router_weight.T,
        expert_ids.T,
        gate_up[0],
        down_proj[0],
    )


def solution(mesh):
    in_specs = (
        P("req", None),
        P("req", None, "tp"),
        P("req", None, None, "tp"),
        P("req"),
        P("tp", None),
        P(),
        P(),
        P("req", None),
        P("req", None, None, "tp"),
        P("req", "tp", None),
    )
    out_specs = P("req", "tp")
    return jax.shard_map(local, mesh=mesh, in_specs=in_specs, out_specs=out_specs, check_vma=False)
```
